32 devices in a mesh: row: 4 (over y, x), col: 8 (over z, core).
Axes of the slice: x: 2, y: 2, z: 4, core: 2. Of those that a mesh axis runs over, the one named last changes fastest.
Arguments:
- features: bfloat16 [16384, 256], P(('col', 'row')), may hold values from -6 to 6
- weight: bfloat16 [256, 256], replicated, may hold values from -0.375 to 0.375
- adjacency: int32 [64, 16, 256, 256], P('row', 'col'), may hold values 0 or 1
- tile_cols: int32 [64, 16], P('row', 'col'), may hold values from 0 to 7
- tile_counts: int32 [64, 8], P('row', 'col'), may hold values from 0 to 2
- cotangent: bfloat16 [16384, 256], P(('row', 'col')), may hold values from -6 to 6
Outputs:
- output: bfloat16 [16384, 256], P(('row', 'col'))
- feature_grad: bfloat16 [16384, 256], P(('col', 'row'))
- weight_grad: float32 [256, 256], replicated
The draws below stay inside these ranges and needn't reach their ends.
Inputs may be any that keep to these rules, and one draw needn't show every extreme that they name: `tile_counts`: slots of a block row at or after its count are not part of the graph.
All inputs are finite; a program needn't handle non-finite values. No bound on the sum of `adjacency` on one device may be relied on, other than what follows from the above.
Results may differ from the reference program's by a relative error of at most 0.0061.
Values may be sent and summed in bfloat16 or wider, within the bound.
A program may use at most 128 MiB of HBM per device.

```python
import jax
import jax.numpy as jnp
from jax import lax

F = 256
TILE = 256
KT = 2
NBR = 64
BCD = 8
NODES = 16384
N_COL = 8


def place_ends(result, key, least, largest):
    longest = result.shape.index(max(result.shape))
    spots = []
    for shift in (0, 1):
        where = [jax.random.randint(jax.random.fold_in(key, axis), (), 0, length) for axis, length in enumerate(result.shape)]
        where[longest] = (where[longest] + shift) % result.shape[longest]
        spots.append(tuple(where))
    return result.at[spots[0]].set(least).at[spots[1]].set(largest)


def steps_of(key, dims, shards, low, top_value):
    factor_of = 1.0
    for position, blocks in shards:
        steps = jax.random.uniform(jax.random.fold_in(jax.random.fold_in(key, 6), position), (blocks,), jnp.float32, low / len(shards), top_value / len(shards))
        factor_of = factor_of * jnp.repeat(jnp.exp(steps), dims[position] // blocks).reshape((-1,) + (1,) * (len(dims) - 1 - position))
    return factor_of


def normal_values(key, dims, deviation, reach, pieces=(), held_as=jnp.bfloat16):
    result = jax.random.normal(key, dims, jnp.float32) * deviation
    if len(pieces) > 0:
        result = steps_of(key, dims, pieces, -0.22, 0.18) * result
    return jnp.clip(result, min=-reach, max=reach).astype(held_as)


def setup_inputs(seed: int = 0) -> dict:
    arg_keys = jax.random.split(jax.random.key(seed), 7)
    return {
        "features": normal_values(arg_keys[0], (NODES, F), 1.0, 6.0, ((0, 32),)),
        "weight": normal_values(arg_keys[1], (F, F), F ** -0.5, 0.375),
        "adjacency": place_ends((jax.random.randint(arg_keys[2], (NBR, N_COL * KT, TILE, TILE), 0, 8) < 1).astype(jnp.int32), jax.random.fold_in(arg_keys[2], 1), 0, 1),
        "tile_cols": place_ends(jax.random.randint(arg_keys[3], (NBR, N_COL * KT), 0, BCD), jax.random.fold_in(arg_keys[3], 1), 0, BCD - 1).astype(jnp.int32),
        "tile_counts": place_ends(jax.random.randint(arg_keys[4], (NBR, N_COL), 0, KT + 1), jax.random.fold_in(arg_keys[4], 1), 0, KT).astype(jnp.int32),
        "cotangent": normal_values(arg_keys[5], (NODES, F), 1.0, 6.0, ((0, 32),)),
    }


def reference(features, weight, adjacency, tile_cols, tile_counts, cotangent):
    hidden = jnp.dot(features, weight, preferred_element_type=jnp.float32).astype(jnp.bfloat16)
    blocks = hidden.reshape(NBR, TILE, F)
    slot_ids = jnp.arange(N_COL * KT)
    owners = slot_ids // KT
    slot_rank = slot_ids % KT

    def forward_row(inputs_row):
        tiles_row, cols_row, counts_row = inputs_row
        usable = slot_rank < counts_row[owners]
        col_blocks = owners * BCD + cols_row
        panels = blocks[col_blocks].astype(jnp.float32)
        panels = jnp.where(usable[:, None, None], panels, jnp.float32(0.0))
        aggregate = jnp.einsum('sij,sjf->if', tiles_row.astype(jnp.float32), panels, precision=lax.Precision.HIGHEST)
        row_sums = lax.optimization_barrier(jnp.sum(tiles_row, axis=2))
        degree = lax.optimization_barrier(jnp.sum(jnp.where(usable[:, None], row_sums, 0), axis=0)).astype(jnp.float32)
        return (aggregate, degree)
    aggregates, degrees = lax.map(forward_row, (adjacency, tile_cols, tile_counts))
    degree = degrees.reshape(NODES)
    inv_root = lax.rsqrt(jnp.float32(1.0) + degree)[:, None]
    preact = aggregates.reshape(NODES, F) * inv_root
    output = jax.nn.silu(preact).astype(jnp.bfloat16)
    sigmoid_v = jax.nn.sigmoid(preact)
    grad_sum = (cotangent.astype(jnp.float32) * sigmoid_v * (1.0 + preact * (1.0 - sigmoid_v)) * inv_root).astype(jnp.bfloat16)
    grad_blocks = grad_sum.reshape(NBR, TILE, F)

    def backward_step(carry, inputs_row):
        tiles_row, cols_row, counts_row, grad_row = inputs_row
        usable = slot_rank < counts_row[owners]
        col_blocks = owners * BCD + cols_row
        contribs = jnp.einsum('sij,if->sjf', tiles_row.astype(jnp.float32), grad_row.astype(jnp.float32), precision=lax.Precision.HIGHEST)
        contribs = jnp.where(usable[:, None, None], contribs, jnp.float32(0.0))
        return (carry.at[col_blocks].add(contribs), None)
    start = jnp.zeros((NBR, TILE, F), jnp.float32)
    summed, unused = lax.scan(backward_step, start, (adjacency, tile_cols, tile_counts, grad_blocks))
    node_grad = summed.reshape(NODES, F).astype(jnp.bfloat16)
    feature_grad = jnp.dot(node_grad, weight.T, preferred_element_type=jnp.float32).astype(jnp.bfloat16)
    weight_grad = jnp.dot(features.T, node_grad, preferred_element_type=jnp.float32) * jnp.float32(1.0 / NODES ** 0.5)
    return (output, feature_grad, weight_grad)
```

```python
import functools
import math

import jax
import jax.numpy as jnp
from jax import lax
from jax.experimental import pallas as pl
from jax.experimental.pallas import tpu as pltpu
from jax.sharding import PartitionSpec as P

MESH = pl.DeviceIdType.MESH
BF = jnp.bfloat16
F32 = jnp.float32


def kernel(
    R, C,
    feats, weight, cols, counts, cot, adj,
    out, fgrad, wterm,
    adj_v, dense, hid, deg, deg_rx, part, pair_tx, pair_rx,
    in_r, in_l, tx_r, tx_l, slab, slab_t, ndt, nd_tx, nd_rx,
    adj_sem, h_send, h_recv, d_send, d_recv, p_send, p_recv,
    r_send, r_recv, l_send, l_recv, gr_send, gr_recv, gl_send, gl_recv,
    s_send, s_recv, n_send, n_recv,
):
    r = lax.axis_index("row")
    c = lax.axis_index("col")
    L = C // 2
    z = c // 2
    k = c % 2
    NB, K, T, _ = adj.shape
    O, F = feats.shape
    N = O * R
    J = N // T
    sib = (r, 2 * z + 1 - k)
    right = (r, c + 2)
    left = (r, c - 2)

    def remote(src, dst, ss, rs, dev):
        return pltpu.make_async_remote_copy(
            src_ref=src, dst_ref=dst, send_sem=ss, recv_sem=rs,
            device_id=dev, device_id_type=MESH)

    def row_peer(d):
        return lax.rem(r + d, R)

    def col_peer(d):
        return lax.rem(c + d, C)

    def load_adj(b):
        return pltpu.make_async_copy(adj.at[b], adj_v.at[b], adj_sem.at[b])

    @pl.loop(0, NB)
    def _(b):
        load_adj(b).start()

    barrier = pltpu.get_barrier_semaphore()
    for d in range(1, R):
        pl.semaphore_signal(barrier, inc=1, device_id=(row_peer(d), c), device_id_type=MESH)
    for d in range(1, C):
        pl.semaphore_signal(barrier, inc=1, device_id=(r, col_peer(d)), device_id_type=MESH)

    hid[pl.ds(pl.multiple_of(r * O, O), O), :] = jnp.dot(
        feats[...], weight[...], preferred_element_type=F32).astype(BF)
    pl.semaphore_wait(barrier, R + C - 2)

    def h_copy(d):
        own = hid.at[pl.ds(pl.multiple_of(r * O, O), O), :]
        return remote(own, own, h_send.at[d - 1], h_recv.at[d - 1], (row_peer(d), c))

    for d in range(1, R):
        h_copy(d).start()

    @pl.loop(0, NB)
    def _(b):
        load_adj(b).wait()
        n = counts[b, 0]
        rows = pl.ds(pl.multiple_of(b * T, T), T)
        vals = []
        for s in range(K):
            live = jnp.where(s < n, 1.0, 0.0).astype(F32)
            v = adj_v[b, s].astype(F32) * live
            vals.append(v)
        total = functools.reduce(lambda a, e: a + e, vals)
        deg[:, rows] = lax.dot_general(
            jnp.ones((8, T), BF), total.astype(BF), (((1,), (1,)), ((), ())),
            preferred_element_type=F32)
        for j in range(J):
            acc = None
            for s in range(K):
                m = jnp.where(cols[b, s] == j, 1.0, 0.0).astype(F32)
                term = vals[s] * m
                acc = term if acc is None else acc + term
            dense[rows, j * T:(j + 1) * T] = acc.astype(BF)

    def d_copy(d):
        src = deg.at[:, pl.ds(pl.multiple_of(col_peer(d) * O, O), O)]
        return remote(src, deg_rx.at[d - 1], d_send.at[d - 1], d_recv.at[d - 1],
                      (r, col_peer(d)))

    for d in range(1, C):
        d_copy(d).start()

    for d in range(1, R):
        h_copy(d).wait_recv()

    per = 2 * O // T

    def p_copy(q):
        return remote(pair_tx.at[q], pair_rx.at[q], p_send.at[q], p_recv.at[q], sib)

    def part_of(q, core):
        return pl.ds(pl.multiple_of((2 * q + core) * O, O), O)

    @pl.loop(0, L)
    def _(i):
        q = jnp.where(i % 2 == 0, L - 1 - i // 2, i // 2)
        for bb in range(per):
            rows = pl.ds(pl.multiple_of((q * per + bb) * T, T), T)
            part[rows, :] = jnp.dot(dense[rows, :], hid[...], preferred_element_type=F32)
        pair_tx[q] = part[part_of(q, 1 - k), :].astype(BF)
        p_copy(q).start()

    def r_copy(q):
        return remote(tx_r.at[q], in_r.at[q], r_send.at[q], r_recv.at[q], right)

    def l_copy(q):
        return remote(tx_l.at[q], in_l.at[q], l_send.at[q], l_recv.at[q], left)

    @pl.loop(0, L - 1)
    def _(i):
        qr = L - 1 - i
        ql = i

        @pl.when(qr > z)
        def _():
            p_copy(qr).wait_recv()
            own = part_of(qr, k)
            part[own, :] += pair_rx[qr].astype(F32)

            @pl.when(z > 0)
            def _():
                r_copy(qr).wait_recv()
                part[own, :] += in_r[qr].astype(F32)

            tx_r[qr] = part[own, :].astype(BF)
            r_copy(qr).start()

        @pl.when(ql < z)
        def _():
            p_copy(ql).wait_recv()
            own = part_of(ql, k)
            part[own, :] += pair_rx[ql].astype(F32)

            @pl.when(z < L - 1)
            def _():
                l_copy(ql).wait_recv()
                part[own, :] += in_l[ql].astype(F32)

            tx_l[ql] = part[own, :].astype(BF)
            l_copy(ql).start()

    for d in range(1, C):
        d_copy(d).wait_recv()
    degree = deg[:, pl.ds(pl.multiple_of(c * O, O), O)]
    for d in range(1, C):
        degree = degree + deg_rx[d - 1]
    inv = lax.rsqrt(1.0 + degree)
    inv = jnp.transpose(jnp.broadcast_to(inv[0:1, :], (128, O)))[:, 0:1]

    mine = part_of(z, k)
    p_copy(z).wait_recv()
    part[mine, :] += pair_rx[z].astype(F32)

    @pl.when(z > 0)
    def _():
        r_copy(z).wait_recv()
        part[mine, :] += in_r[z].astype(F32)

    @pl.when(z < L - 1)
    def _():
        l_copy(z).wait_recv()
        part[mine, :] += in_l[z].astype(F32)

    pre = part[mine, :] * inv
    sig = jax.nn.sigmoid(pre)
    out[...] = (pre * sig).astype(BF)
    slab[mine, :] = (cot[...].astype(F32) * sig * (1.0 + pre * (1.0 - sig)) * inv).astype(BF)

    def s_copy(p):
        ref = slab.at[part_of(p, k), :]
        return remote(ref, ref, s_send.at[p], s_recv.at[p], sib)

    def s_wait(p):
        ref = slab.at[part_of(p, 1 - k), :]
        remote(ref, ref, s_send.at[p], s_recv.at[p], sib).wait_recv()

    def gr_copy(i, p):
        ref = slab.at[part_of(p, k), :]
        return remote(ref, ref, gr_send.at[i], gr_recv.at[i], right)

    def gl_copy(i, p):
        ref = slab.at[part_of(p, k), :]
        return remote(ref, ref, gl_send.at[i], gl_recv.at[i], left)

    @pl.when(z < L - 1)
    def _():
        gr_copy(0, z).start()

    @pl.when(z > 0)
    def _():
        gl_copy(0, z).start()

    s_copy(z).start()
    CH = 512 if N % 512 == 0 else T
    ndt[...] = jnp.zeros_like(ndt)

    def accumulate(p):
        rows = pl.ds(pl.multiple_of(2 * p * O, 2 * O), 2 * O)
        slab_t[...] = jnp.transpose(slab[rows, :].astype(F32)).astype(BF)

        @pl.loop(0, N // CH)
        def _(j):
            cc = pl.ds(pl.multiple_of(j * CH, CH), CH)
            ndt[:, cc] += jnp.dot(slab_t[...], dense[rows, cc], preferred_element_type=F32)

    s_wait(z)
    accumulate(z)

    @pl.loop(1, L)
    def _(i):
        pr = z - i
        pln = z + i

        @pl.when(pr >= 0)
        def _():
            gr_copy(i - 1, pr).wait_recv()

            @pl.when(z < L - 1)
            def _():
                gr_copy(i, pr).start()
            s_copy(pr).start()

        @pl.when(pln <= L - 1)
        def _():
            gl_copy(i - 1, pln).wait_recv()

            @pl.when(z > 0)
            def _():
                gl_copy(i, pln).start()
            s_copy(pln).start()

        @pl.when(pr >= 0)
        def _():
            s_wait(pr)
            accumulate(pr)

        @pl.when(pln <= L - 1)
        def _():
            s_wait(pln)
            accumulate(pln)

    def n_copy(d):
        return remote(nd_tx.at[d - 1], nd_rx.at[d - 1], n_send.at[d - 1], n_recv.at[d - 1],
                      (row_peer(d), c))

    for d in range(1, R):
        nd_tx[d - 1] = ndt[:, pl.ds(pl.multiple_of(row_peer(d) * O, O), O)].astype(BF)
        n_copy(d).start()
    total = ndt[:, pl.ds(pl.multiple_of(r * O, O), O)]
    for d in range(1, R):
        n_copy(d).wait_recv()
        total = total + nd_rx[d - 1].astype(F32)
    node = jnp.transpose(total).astype(BF)
    wterm[...] = lax.dot_general(
        feats[...], node, (((0,), (0,)), ((), ())), preferred_element_type=F32)
    fgrad[...] = lax.dot_general(
        node, weight[...], (((1,), (1,)), ((), ())), preferred_element_type=F32).astype(BF)

    for d in range(1, R):
        h_copy(d).wait_send()
        n_copy(d).wait_send()
    for d in range(1, C):
        d_copy(d).wait_send()

    @pl.loop(0, L)
    def _(q):
        p_copy(q).wait_send()
        s_copy(q).wait_send()

        @pl.when(q > z)
        def _():
            r_copy(q).wait_send()

        @pl.when(q < z)
        def _():
            l_copy(q).wait_send()

        @pl.when((q <= z) & (z < L - 1))
        def _():
            gr_copy(q, z - q).wait_send()

        @pl.when((q <= L - 1 - z) & (z > 0))
        def _():
            gl_copy(q, z + q).wait_send()


def shards(features, weight, adjacency, tile_cols, tile_counts, cotangent):
    R = lax.axis_size("row")
    C = lax.axis_size("col")
    L = C // 2
    NB, K, T, _ = adjacency.shape
    O, F = features.shape
    N = O * R
    M = NB * T
    vmem = pl.BlockSpec(memory_space=pltpu.VMEM)
    smem = pl.BlockSpec(memory_space=pltpu.SMEM)
    dma = pltpu.SemaphoreType.DMA
    scratch = [
        pltpu.VMEM((NB, K, T, T), jnp.int32),
        pltpu.VMEM((M, N), BF),
        pltpu.VMEM((N, F), BF),
        pltpu.VMEM((8, M), F32),
        pltpu.VMEM((C - 1, 8, O), F32),
        pltpu.VMEM((M, F), F32),
        pltpu.VMEM((L, O, F), BF),
        pltpu.VMEM((L, O, F), BF),
        pltpu.VMEM((L, O, F), BF),
        pltpu.VMEM((L, O, F), BF),
        pltpu.VMEM((L, O, F), BF),
        pltpu.VMEM((L, O, F), BF),
        pltpu.VMEM((M, F), BF),
        pltpu.VMEM((F, 2 * O), BF),
        pltpu.VMEM((F, N), F32),
        pltpu.VMEM((R - 1, F, O), BF),
        pltpu.VMEM((R - 1, F, O), BF),
        dma((NB,)),
        dma((R - 1,)), dma((R - 1,)),
        dma((C - 1,)), dma((C - 1,)),
        dma((L,)), dma((L,)),
        dma((L,)), dma((L,)),
        dma((L,)), dma((L,)),
        dma((L,)), dma((L,)),
        dma((L,)), dma((L,)),
        dma((L,)), dma((L,)),
        dma((R - 1,)), dma((R - 1,)),
    ]
    out, fgrad, wterm = pl.pallas_call(
        functools.partial(kernel, R, C),
        out_shape=(
            jax.ShapeDtypeStruct((O, F), BF),
            jax.ShapeDtypeStruct((O, F), BF),
            jax.ShapeDtypeStruct((F, F), F32),
        ),
        in_specs=[vmem, vmem, smem, smem, vmem, pl.BlockSpec(memory_space=pl.ANY)],
        out_specs=(vmem, vmem, vmem),
        scratch_shapes=scratch,
        compiler_params=pltpu.CompilerParams(
            collective_id=0, has_side_effects=True, vmem_limit_bytes=60 * 1024 * 1024),
    )(features, weight, tile_cols, tile_counts, cotangent, adjacency)
    node_total = O * R * C
    wgrad = lax.psum(wterm, ("row", "col")) * jnp.float32(1.0 / math.sqrt(node_total))
    return out, fgrad, wgrad


def solution(mesh):
    placed = (
        P(("col", "row"), None),
        P(),
        P("row", "col", None, None),
        P("row", "col"),
        P("row", "col"),
        P(("row", "col"), None),
    )
    return jax.shard_map(
        shards,
        mesh=mesh,
        in_specs=placed,
        out_specs=(P(("row", "col"), None), P(("col", "row"), None), P()),
        check_vma=False,
    )
```

```python
import functools
import math

import jax
import jax.numpy as jnp
from jax import lax
from jax.experimental import pallas as pl
from jax.experimental.pallas import tpu as pltpu
from jax.sharding import PartitionSpec as P

MESH = pl.DeviceIdType.MESH
BF = jnp.bfloat16
F32 = jnp.float32


def kernel(
    R, C, scale,
    feats, weight, cols, counts, cot, adj,
    out, fgrad, wgrad,
    adj_v, dense, hid, deg, deg_rx, part, pair_tx, pair_rx,
    in_r, in_l, tx_r, tx_l, slab, slab_t, ndt, nd_tx, nd_rx,
    w_term, w_rx, w_cur, w_in, w_all,
    adj_sem, h_send, h_recv, d_send, d_recv, p_send, p_recv,
    r_send, r_recv, l_send, l_recv, gr_send, gr_recv, gl_send, gl_recv,
    s_send, s_recv, n_send, n_recv,
    w_send, w_recv, b_send, b_recv, a_send, a_recv,
):
    r = lax.axis_index("row")
    c = lax.axis_index("col")
    L = C // 2
    z = c // 2
    k = c % 2
    NB, K, T, _ = adj.shape
    O, F = feats.shape
    N = O * R
    J = N // T
    sib = (r, 2 * z + 1 - k)
    right = (r, c + 2)
    left = (r, c - 2)

    def remote(src, dst, ss, rs, dev):
        return pltpu.make_async_remote_copy(
            src_ref=src, dst_ref=dst, send_sem=ss, recv_sem=rs,
            device_id=dev, device_id_type=MESH)

    def row_peer(d):
        return lax.rem(r + d, R)

    def col_peer(d):
        return lax.rem(c + d, C)

    def load_adj(b):
        return pltpu.make_async_copy(adj.at[b], adj_v.at[b], adj_sem.at[b])

    @pl.loop(0, NB)
    def _(b):
        load_adj(b).start()

    barrier = pltpu.get_barrier_semaphore()
    for d in range(1, R):
        pl.semaphore_signal(barrier, inc=1, device_id=(row_peer(d), c), device_id_type=MESH)
    for d in range(1, C):
        pl.semaphore_signal(barrier, inc=1, device_id=(r, col_peer(d)), device_id_type=MESH)

    hid[pl.ds(pl.multiple_of(r * O, O), O), :] = jnp.dot(
        feats[...], weight[...], preferred_element_type=F32).astype(BF)
    pl.semaphore_wait(barrier, R + C - 2)

    def h_copy(d):
        own = hid.at[pl.ds(pl.multiple_of(r * O, O), O), :]
        return remote(own, own, h_send.at[d - 1], h_recv.at[d - 1], (row_peer(d), c))

    for d in range(1, R):
        h_copy(d).start()

    @pl.loop(0, NB)
    def _(b):
        load_adj(b).wait()
        n = counts[b, 0]
        rows = pl.ds(pl.multiple_of(b * T, T), T)
        vals = []
        for s in range(K):
            live = jnp.where(s < n, 1.0, 0.0).astype(F32)
            v = adj_v[b, s].astype(F32) * live
            vals.append(v)
        total = functools.reduce(lambda a, e: a + e, vals)
        deg[:, rows] = lax.dot_general(
            jnp.ones((8, T), BF), total.astype(BF), (((1,), (1,)), ((), ())),
            preferred_element_type=F32)
        for j in range(J):
            acc = None
            for s in range(K):
                m = jnp.where(cols[b, s] == j, 1.0, 0.0).astype(F32)
                term = vals[s] * m
                acc = term if acc is None else acc + term
            dense[rows, j * T:(j + 1) * T] = acc.astype(BF)

    def d_copy(d):
        src = deg.at[:, pl.ds(pl.multiple_of(col_peer(d) * O, O), O)]
        return remote(src, deg_rx.at[d - 1], d_send.at[d - 1], d_recv.at[d - 1],
                      (r, col_peer(d)))

    for d in range(1, C):
        d_copy(d).start()

    for d in range(1, R):
        h_copy(d).wait_recv()

    per = 2 * O // T

    def p_copy(q):
        return remote(pair_tx.at[q], pair_rx.at[q], p_send.at[q], p_recv.at[q], sib)

    def part_of(q, core):
        return pl.ds(pl.multiple_of((2 * q + core) * O, O), O)

    @pl.loop(0, L)
    def _(i):
        q = jnp.where(i % 2 == 0, L - 1 - i // 2, i // 2)
        for bb in range(per):
            rows = pl.ds(pl.multiple_of((q * per + bb) * T, T), T)
            part[rows, :] = jnp.dot(dense[rows, :], hid[...], preferred_element_type=F32)
        pair_tx[q] = part[part_of(q, 1 - k), :].astype(BF)
        p_copy(q).start()

    def r_copy(q):
        return remote(tx_r.at[q], in_r.at[q], r_send.at[q], r_recv.at[q], right)

    def l_copy(q):
        return remote(tx_l.at[q], in_l.at[q], l_send.at[q], l_recv.at[q], left)

    @pl.loop(0, L - 1)
    def _(i):
        qr = L - 1 - i
        ql = i

        @pl.when(qr > z)
        def _():
            p_copy(qr).wait_recv()
            own = part_of(qr, k)
            part[own, :] += pair_rx[qr].astype(F32)

            @pl.when(z > 0)
            def _():
                r_copy(qr).wait_recv()
                part[own, :] += in_r[qr].astype(F32)

            tx_r[qr] = part[own, :].astype(BF)
            r_copy(qr).start()

        @pl.when(ql < z)
        def _():
            p_copy(ql).wait_recv()
            own = part_of(ql, k)
            part[own, :] += pair_rx[ql].astype(F32)

            @pl.when(z < L - 1)
            def _():
                l_copy(ql).wait_recv()
                part[own, :] += in_l[ql].astype(F32)

            tx_l[ql] = part[own, :].astype(BF)
            l_copy(ql).start()

    for d in range(1, C):
        d_copy(d).wait_recv()
    degree = deg[:, pl.ds(pl.multiple_of(c * O, O), O)]
    for d in range(1, C):
        degree = degree + deg_rx[d - 1]
    inv = lax.rsqrt(1.0 + degree)
    inv = jnp.transpose(jnp.broadcast_to(inv[0:1, :], (128, O)))[:, 0:1]

    mine = part_of(z, k)
    p_copy(z).wait_recv()
    part[mine, :] += pair_rx[z].astype(F32)

    @pl.when(z > 0)
    def _():
        r_copy(z).wait_recv()
        part[mine, :] += in_r[z].astype(F32)

    @pl.when(z < L - 1)
    def _():
        l_copy(z).wait_recv()
        part[mine, :] += in_l[z].astype(F32)

    pre = part[mine, :] * inv
    sig = jax.nn.sigmoid(pre)
    out[...] = (pre * sig).astype(BF)
    slab[mine, :] = (cot[...].astype(F32) * sig * (1.0 + pre * (1.0 - sig)) * inv).astype(BF)

    def s_copy(p):
        ref = slab.at[part_of(p, k), :]
        return remote(ref, ref, s_send.at[p], s_recv.at[p], sib)

    def s_wait(p):
        ref = slab.at[part_of(p, 1 - k), :]
        remote(ref, ref, s_send.at[p], s_recv.at[p], sib).wait_recv()

    def gr_copy(i, p):
        ref = slab.at[part_of(p, k), :]
        return remote(ref, ref, gr_send.at[i], gr_recv.at[i], right)

    def gl_copy(i, p):
        ref = slab.at[part_of(p, k), :]
        return remote(ref, ref, gl_send.at[i], gl_recv.at[i], left)

    @pl.when(z < L - 1)
    def _():
        gr_copy(0, z).start()

    @pl.when(z > 0)
    def _():
        gl_copy(0, z).start()

    s_copy(z).start()
    CH = 512 if N % 512 == 0 else T
    ndt[...] = jnp.zeros_like(ndt)

    def accumulate(p):
        rows = pl.ds(pl.multiple_of(2 * p * O, 2 * O), 2 * O)
        slab_t[...] = jnp.transpose(slab[rows, :].astype(F32)).astype(BF)

        @pl.loop(0, N // CH)
        def _(j):
            cc = pl.ds(pl.multiple_of(j * CH, CH), CH)
            ndt[:, cc] += jnp.dot(slab_t[...], dense[rows, cc], preferred_element_type=F32)

    s_wait(z)
    accumulate(z)

    @pl.loop(1, L)
    def _(i):
        pr = z - i
        pln = z + i

        @pl.when(pr >= 0)
        def _():
            gr_copy(i - 1, pr).wait_recv()

            @pl.when(z < L - 1)
            def _():
                gr_copy(i, pr).start()
            s_copy(pr).start()

        @pl.when(pln <= L - 1)
        def _():
            gl_copy(i - 1, pln).wait_recv()

            @pl.when(z > 0)
            def _():
                gl_copy(i, pln).start()
            s_copy(pln).start()

        @pl.when(pr >= 0)
        def _():
            s_wait(pr)
            accumulate(pr)

        @pl.when(pln <= L - 1)
        def _():
            s_wait(pln)
            accumulate(pln)

    def n_copy(d):
        return remote(nd_tx.at[d - 1], nd_rx.at[d - 1], n_send.at[d - 1], n_recv.at[d - 1],
                      (row_peer(d), c))

    for d in range(1, R):
        nd_tx[d - 1] = ndt[:, pl.ds(pl.multiple_of(row_peer(d) * O, O), O)].astype(BF)
        n_copy(d).start()
    total = ndt[:, pl.ds(pl.multiple_of(r * O, O), O)]
    for d in range(1, R):
        n_copy(d).wait_recv()
        total = total + nd_rx[d - 1].astype(F32)
    node = jnp.transpose(total).astype(BF)
    w_term[...] = lax.dot_general(
        feats[...], node, (((0,), (0,)), ((), ())), preferred_element_type=F32)

    G = F // R
    steps = C.bit_length() - 1

    def w_rows(i):
        return pl.ds(pl.multiple_of(i * G, G), G)

    def w_copy(d):
        return remote(w_term.at[w_rows(row_peer(d)), :], w_rx.at[d - 1],
                      w_send.at[d - 1], w_recv.at[d - 1], (row_peer(d), c))

    def b_copy(s):
        w = 1 << s
        partner = c + w - 2 * w * ((c // w) % 2)
        return remote(w_cur.at[s], w_in.at[s], b_send.at[s], b_recv.at[s], (r, partner))

    def a_copy(d):
        ref = w_all.at[w_rows(r), :]
        return remote(ref, ref, a_send.at[d - 1], a_recv.at[d - 1], (row_peer(d), c))

    for d in range(1, R):
        w_copy(d).start()
    fgrad[...] = lax.dot_general(
        node, weight[...], (((1,), (1,)), ((), ())), preferred_element_type=F32).astype(BF)

    wsum = w_term[w_rows(r), :]
    for d in range(1, R):
        w_copy(d).wait_recv()
        wsum = wsum + w_rx[d - 1]
    for s in range(steps):
        w_cur[s] = wsum
        b_copy(s).start()
        b_copy(s).wait_recv()
        wsum = wsum + w_in[s]
    w_all[w_rows(r), :] = wsum * scale
    for d in range(1, R):
        a_copy(d).start()
    for d in range(1, R):
        a_copy(d).wait_recv()
    wgrad[...] = w_all[...]

    for s in range(steps):
        b_copy(s).wait_send()
    for d in range(1, R):
        w_copy(d).wait_send()
        a_copy(d).wait_send()
    for d in range(1, R):
        h_copy(d).wait_send()
        n_copy(d).wait_send()
    for d in range(1, C):
        d_copy(d).wait_send()

    @pl.loop(0, L)
    def _(q):
        p_copy(q).wait_send()
        s_copy(q).wait_send()

        @pl.when(q > z)
        def _():
            r_copy(q).wait_send()

        @pl.when(q < z)
        def _():
            l_copy(q).wait_send()

        @pl.when((q <= z) & (z < L - 1))
        def _():
            gr_copy(q, z - q).wait_send()

        @pl.when((q <= L - 1 - z) & (z > 0))
        def _():
            gl_copy(q, z + q).wait_send()


def shards(features, weight, adjacency, tile_cols, tile_counts, cotangent):
    R = lax.axis_size("row")
    C = lax.axis_size("col")
    L = C // 2
    NB, K, T, _ = adjacency.shape
    O, F = features.shape
    N = O * R
    M = NB * T
    G = F // R
    steps = C.bit_length() - 1
    scale = 1.0 / math.sqrt(O * R * C)
    vmem = pl.BlockSpec(memory_space=pltpu.VMEM)
    smem = pl.BlockSpec(memory_space=pltpu.SMEM)
    dma = pltpu.SemaphoreType.DMA
    scratch = [
        pltpu.VMEM((NB, K, T, T), jnp.int32),
        pltpu.VMEM((M, N), BF),
        pltpu.VMEM((N, F), BF),
        pltpu.VMEM((8, M), F32),
        pltpu.VMEM((C - 1, 8, O), F32),
        pltpu.VMEM((M, F), F32),
        pltpu.VMEM((L, O, F), BF),
        pltpu.VMEM((L, O, F), BF),
        pltpu.VMEM((L, O, F), BF),
        pltpu.VMEM((L, O, F), BF),
        pltpu.VMEM((L, O, F), BF),
        pltpu.VMEM((L, O, F), BF),
        pltpu.VMEM((M, F), BF),
        pltpu.VMEM((F, 2 * O), BF),
        pltpu.VMEM((F, N), F32),
        pltpu.VMEM((R - 1, F, O), BF),
        pltpu.VMEM((R - 1, F, O), BF),
        pltpu.VMEM((F, F), F32),
        pltpu.VMEM((R - 1, G, F), F32),
        pltpu.VMEM((steps, G, F), F32),
        pltpu.VMEM((steps, G, F), F32),
        pltpu.VMEM((F, F), F32),
        dma((NB,)),
        dma((R - 1,)), dma((R - 1,)),
        dma((C - 1,)), dma((C - 1,)),
        dma((L,)), dma((L,)),
        dma((L,)), dma((L,)),
        dma((L,)), dma((L,)),
        dma((L,)), dma((L,)),
        dma((L,)), dma((L,)),
        dma((L,)), dma((L,)),
        dma((R - 1,)), dma((R - 1,)),
        dma((R - 1,)), dma((R - 1,)),
        dma((steps,)), dma((steps,)),
        dma((R - 1,)), dma((R - 1,)),
    ]
    out, fgrad, wgrad = pl.pallas_call(
        functools.partial(kernel, R, C, scale),
        out_shape=(
            jax.ShapeDtypeStruct((O, F), BF),
            jax.ShapeDtypeStruct((O, F), BF),
            jax.ShapeDtypeStruct((F, F), F32),
        ),
        in_specs=[vmem, vmem, smem, smem, vmem, pl.BlockSpec(memory_space=pl.ANY)],
        out_specs=(vmem, vmem, vmem),
        scratch_shapes=scratch,
        compiler_params=pltpu.CompilerParams(
            collective_id=0, has_side_effects=True, vmem_limit_bytes=60 * 1024 * 1024),
    )(features, weight, tile_cols, tile_counts, cotangent, adjacency)
    return out, fgrad, wgrad


def solution(mesh):
    placed = (
        P(("col", "row"), None),
        P(),
        P("row", "col", None, None),
        P("row", "col"),
        P("row", "col"),
        P(("row", "col"), None),
    )
    return jax.shard_map(
        shards,
        mesh=mesh,
        in_specs=placed,
        out_specs=(P(("row", "col"), None), P(("col", "row"), None), P()),
        check_vma=False,
    )
```

```python
import functools
import math

import jax
import jax.numpy as jnp
from jax import lax
from jax.experimental import pallas as pl
from jax.experimental.pallas import tpu as pltpu
from jax.sharding import PartitionSpec as P

MESH = pl.DeviceIdType.MESH
BF = jnp.bfloat16
F32 = jnp.float32
NH = 2


def kernel(
    R, C, scale,
    feats, weight, cols, counts, cot, adj,
    out, fgrad, wgrad,
    adj_v, dense, hid, deg, deg_rx, part, pair_tx, pair_rx,
    in_r, in_l, tx_r, tx_l, slab, slab_t, ndt, nd_tx, nd_rx,
    w_term, w_rx, w_cur, w_in, w_all,
    adj_sem, h_send, h_recv, d_send, d_recv, p_send, p_recv,
    r_send, r_recv, l_send, l_recv, gr_send, gr_recv, gl_send, gl_recv,
    s_send, s_recv, n_send, n_recv,
    w_send, w_recv, b_send, b_recv, a_send, a_recv,
):
    r = lax.axis_index("row")
    c = lax.axis_index("col")
    L = C // 2
    z = c // 2
    k = c % 2
    NB, K, T, _ = adj.shape
    O, F = feats.shape
    N = O * R
    J = N // T
    HF = F // NH

    def cs(h):
        return slice(h * HF, (h + 1) * HF)

    sib = (r, 2 * z + 1 - k)
    right = (r, c + 2)
    left = (r, c - 2)

    def remote(src, dst, ss, rs, dev):
        return pltpu.make_async_remote_copy(
            src_ref=src, dst_ref=dst, send_sem=ss, recv_sem=rs,
            device_id=dev, device_id_type=MESH)

    def row_peer(d):
        return lax.rem(r + d, R)

    def col_peer(d):
        return lax.rem(c + d, C)

    def load_adj(b):
        return pltpu.make_async_copy(adj.at[b], adj_v.at[b], adj_sem.at[b])

    @pl.loop(0, NB)
    def _(b):
        load_adj(b).start()

    barrier = pltpu.get_barrier_semaphore()
    for d in range(1, R):
        pl.semaphore_signal(barrier, inc=1, device_id=(row_peer(d), c), device_id_type=MESH)
    for d in range(1, C):
        pl.semaphore_signal(barrier, inc=1, device_id=(r, col_peer(d)), device_id_type=MESH)

    hid[pl.ds(pl.multiple_of(r * O, O), O), :] = jnp.dot(
        feats[...], weight[...], preferred_element_type=F32).astype(BF)
    pl.semaphore_wait(barrier, R + C - 2)

    def h_copy(d):
        own = hid.at[pl.ds(pl.multiple_of(r * O, O), O), :]
        return remote(own, own, h_send.at[d - 1], h_recv.at[d - 1], (row_peer(d), c))

    for d in range(1, R):
        h_copy(d).start()

    @pl.loop(0, NB)
    def _(b):
        load_adj(b).wait()
        n = counts[b, 0]
        rows = pl.ds(pl.multiple_of(b * T, T), T)
        vals = []
        for s in range(K):
            live = jnp.where(s < n, 1.0, 0.0).astype(F32)
            v = adj_v[b, s].astype(F32) * live
            vals.append(v)
        total = functools.reduce(lambda a, e: a + e, vals)
        deg[:, rows] = lax.dot_general(
            jnp.ones((8, T), BF), total.astype(BF), (((1,), (1,)), ((), ())),
            preferred_element_type=F32)
        for j in range(J):
            acc = None
            for s in range(K):
                m = jnp.where(cols[b, s] == j, 1.0, 0.0).astype(F32)
                term = vals[s] * m
                acc = term if acc is None else acc + term
            dense[rows, j * T:(j + 1) * T] = acc.astype(BF)

    def d_copy(d):
        src = deg.at[:, pl.ds(pl.multiple_of(col_peer(d) * O, O), O)]
        return remote(src, deg_rx.at[d - 1], d_send.at[d - 1], d_recv.at[d - 1],
                      (r, col_peer(d)))

    for d in range(1, C):
        d_copy(d).start()

    for d in range(1, R):
        h_copy(d).wait_recv()

    per = 2 * O // T

    def p_copy(q, h):
        return remote(pair_tx.at[q, :, cs(h)], pair_rx.at[q, :, cs(h)],
                      p_send.at[h, q], p_recv.at[h, q], sib)

    def part_of(q, core):
        return pl.ds(pl.multiple_of((2 * q + core) * O, O), O)

    @pl.loop(0, L)
    def _(i):
        q = jnp.where(i % 2 == 0, L - 1 - i // 2, i // 2)
        for bb in range(per):
            rows = pl.ds(pl.multiple_of((q * per + bb) * T, T), T)
            part[rows, :] = jnp.dot(dense[rows, :], hid[...], preferred_element_type=F32)
        pair_tx[q] = part[part_of(q, 1 - k), :].astype(BF)
        for h in range(NH):
            p_copy(q, h).start()

    def r_copy(q, h):
        return remote(tx_r.at[q, :, cs(h)], in_r.at[q, :, cs(h)],
                      r_send.at[h, q], r_recv.at[h, q], right)

    def l_copy(q, h):
        return remote(tx_l.at[q, :, cs(h)], in_l.at[q, :, cs(h)],
                      l_send.at[h, q], l_recv.at[h, q], left)

    def sum_step(i, h):
        qr = L - 1 - i
        ql = i

        @pl.when(qr > z)
        def _():
            p_copy(qr, h).wait_recv()
            own = part_of(qr, k)
            part[own, cs(h)] += pair_rx[qr, :, cs(h)].astype(F32)

            @pl.when(z > 0)
            def _():
                r_copy(qr, h).wait_recv()
                part[own, cs(h)] += in_r[qr, :, cs(h)].astype(F32)

            tx_r[qr, :, cs(h)] = part[own, cs(h)].astype(BF)
            r_copy(qr, h).start()

        @pl.when(ql < z)
        def _():
            p_copy(ql, h).wait_recv()
            own = part_of(ql, k)
            part[own, cs(h)] += pair_rx[ql, :, cs(h)].astype(F32)

            @pl.when(z < L - 1)
            def _():
                l_copy(ql, h).wait_recv()
                part[own, cs(h)] += in_l[ql, :, cs(h)].astype(F32)

            tx_l[ql, :, cs(h)] = part[own, cs(h)].astype(BF)
            l_copy(ql, h).start()

    @pl.loop(0, L - 1)
    def _(i):
        sum_step(i, 0)

    for d in range(1, C):
        d_copy(d).wait_recv()
    degree = deg[:, pl.ds(pl.multiple_of(c * O, O), O)]
    for d in range(1, C):
        degree = degree + deg_rx[d - 1]
    inv = lax.rsqrt(1.0 + degree)
    inv = jnp.transpose(jnp.broadcast_to(inv[0:1, :], (128, O)))[:, 0:1]

    mine = part_of(z, k)

    def finish(h):
        p_copy(z, h).wait_recv()
        part[mine, cs(h)] += pair_rx[z, :, cs(h)].astype(F32)

        @pl.when(z > 0)
        def _():
            r_copy(z, h).wait_recv()
            part[mine, cs(h)] += in_r[z, :, cs(h)].astype(F32)

        @pl.when(z < L - 1)
        def _():
            l_copy(z, h).wait_recv()
            part[mine, cs(h)] += in_l[z, :, cs(h)].astype(F32)

        pre = part[mine, cs(h)] * inv
        sig = jax.nn.sigmoid(pre)
        out[:, cs(h)] = (pre * sig).astype(BF)
        slab[mine, cs(h)] = (
            cot[:, cs(h)].astype(F32) * sig * (1.0 + pre * (1.0 - sig)) * inv).astype(BF)

    def s_copy(p, h):
        ref = slab.at[part_of(p, k), cs(h)]
        return remote(ref, ref, s_send.at[h, p], s_recv.at[h, p], sib)

    def s_wait(p, h):
        ref = slab.at[part_of(p, 1 - k), cs(h)]
        remote(ref, ref, s_send.at[h, p], s_recv.at[h, p], sib).wait_recv()

    def gr_copy(i, p, h):
        ref = slab.at[part_of(p, k), cs(h)]
        return remote(ref, ref, gr_send.at[h, i], gr_recv.at[h, i], right)

    def gl_copy(i, p, h):
        ref = slab.at[part_of(p, k), cs(h)]
        return remote(ref, ref, gl_send.at[h, i], gl_recv.at[h, i], left)

    def spread(h):
        @pl.when(z < L - 1)
        def _():
            gr_copy(0, z, h).start()

        @pl.when(z > 0)
        def _():
            gl_copy(0, z, h).start()

        s_copy(z, h).start()

    def forward(i, h):
        pr = z - i
        pln = z + i

        @pl.when(pr >= 0)
        def _():
            gr_copy(i - 1, pr, h).wait_recv()

            @pl.when(z < L - 1)
            def _():
                gr_copy(i, pr, h).start()
            s_copy(pr, h).start()

        @pl.when(pln <= L - 1)
        def _():
            gl_copy(i - 1, pln, h).wait_recv()

            @pl.when(z > 0)
            def _():
                gl_copy(i, pln, h).start()
            s_copy(pln, h).start()

    CH = 512 if N % 512 == 0 else T

    def accumulate(p, h, first=False):
        rows = pl.ds(pl.multiple_of(2 * p * O, 2 * O), 2 * O)
        s_wait(p, h)
        slab_t[...] = jnp.transpose(slab[rows, cs(h)].astype(F32)).astype(BF)

        @pl.loop(0, N // CH)
        def _(j):
            cc = pl.ds(pl.multiple_of(j * CH, CH), CH)
            term = jnp.dot(slab_t[...], dense[rows, cc], preferred_element_type=F32)
            if first:
                ndt[cs(h), cc] = term
            else:
                ndt[cs(h), cc] += term

    def both(i, h):
        @pl.when(z - i >= 0)
        def _():
            accumulate(z - i, h)

        @pl.when(z + i <= L - 1)
        def _():
            accumulate(z + i, h)

    def n_copy(d, h):
        return remote(nd_tx.at[d - 1, cs(h), :], nd_rx.at[d - 1, cs(h), :],
                      n_send.at[h, d - 1], n_recv.at[h, d - 1], (row_peer(d), c))

    def scatter(h):
        for d in range(1, R):
            there = pl.ds(pl.multiple_of(row_peer(d) * O, O), O)
            nd_tx[d - 1, cs(h), :] = ndt[cs(h), there].astype(BF)
            n_copy(d, h).start()

    finish(0)
    spread(0)

    @pl.loop(0, L - 1)
    def _(i):
        sum_step(i, 1)
        forward(i + 1, 0)

    finish(1)
    spread(1)
    accumulate(z, 0, True)

    @pl.loop(1, L)
    def _(i):
        forward(i, 1)
        both(i, 0)

    scatter(0)
    accumulate(z, 1, True)

    @pl.loop(1, L)
    def _(i):
        both(i, 1)

    scatter(1)

    total = ndt[:, pl.ds(pl.multiple_of(r * O, O), O)]
    for d in range(1, R):
        for h in range(NH):
            n_copy(d, h).wait_recv()
        total = total + nd_rx[d - 1].astype(F32)
    node = jnp.transpose(total).astype(BF)
    w_term[...] = lax.dot_general(
        feats[...], node, (((0,), (0,)), ((), ())), preferred_element_type=F32)

    G = F // R
    steps = C.bit_length() - 1

    def w_rows(i):
        return pl.ds(pl.multiple_of(i * G, G), G)

    def w_copy(d):
        return remote(w_term.at[w_rows(row_peer(d)), :], w_rx.at[d - 1],
                      w_send.at[d - 1], w_recv.at[d - 1], (row_peer(d), c))

    def b_copy(s):
        w = 1 << s
        partner = c + w - 2 * w * ((c // w) % 2)
        return remote(w_cur.at[s], w_in.at[s], b_send.at[s], b_recv.at[s], (r, partner))

    def a_copy(d):
        ref = w_all.at[w_rows(r), :]
        return remote(ref, ref, a_send.at[d - 1], a_recv.at[d - 1], (row_peer(d), c))

    for d in range(1, R):
        w_copy(d).start()
    fgrad[...] = lax.dot_general(
        node, weight[...], (((1,), (1,)), ((), ())), preferred_element_type=F32).astype(BF)

    wsum = w_term[w_rows(r), :]
    for d in range(1, R):
        w_copy(d).wait_recv()
        wsum = wsum + w_rx[d - 1]
    for s in range(steps):
        w_cur[s] = wsum
        b_copy(s).start()
        b_copy(s).wait_recv()
        wsum = wsum + w_in[s]
    w_all[w_rows(r), :] = wsum * scale
    for d in range(1, R):
        a_copy(d).start()
    for d in range(1, R):
        a_copy(d).wait_recv()
    wgrad[...] = w_all[...]

    def drain(q, h):
        p_copy(q, h).wait_send()
        s_copy(q, h).wait_send()

        @pl.when(q > z)
        def _():
            r_copy(q, h).wait_send()

        @pl.when(q < z)
        def _():
            l_copy(q, h).wait_send()

        @pl.when((q <= z) & (z < L - 1))
        def _():
            gr_copy(q, z - q, h).wait_send()

        @pl.when((q <= L - 1 - z) & (z > 0))
        def _():
            gl_copy(q, z + q, h).wait_send()

    for s in range(steps):
        b_copy(s).wait_send()
    for d in range(1, R):
        w_copy(d).wait_send()
        a_copy(d).wait_send()
    for d in range(1, R):
        h_copy(d).wait_send()
        for h in range(NH):
            n_copy(d, h).wait_send()
    for d in range(1, C):
        d_copy(d).wait_send()

    @pl.loop(0, L)
    def _(q):
        for h in range(NH):
            drain(q, h)


def shards(features, weight, adjacency, tile_cols, tile_counts, cotangent):
    R = lax.axis_size("row")
    C = lax.axis_size("col")
    L = C // 2
    NB, K, T, _ = adjacency.shape
    O, F = features.shape
    N = O * R
    M = NB * T
    G = F // R
    steps = C.bit_length() - 1
    scale = 1.0 / math.sqrt(O * R * C)
    vmem = pl.BlockSpec(memory_space=pltpu.VMEM)
    smem = pl.BlockSpec(memory_space=pltpu.SMEM)
    dma = pltpu.SemaphoreType.DMA
    scratch = [
        pltpu.VMEM((NB, K, T, T), jnp.int32),
        pltpu.VMEM((M, N), BF),
        pltpu.VMEM((N, F), BF),
        pltpu.VMEM((8, M), F32),
        pltpu.VMEM((C - 1, 8, O), F32),
        pltpu.VMEM((M, F), F32),
        pltpu.VMEM((L, O, F), BF),
        pltpu.VMEM((L, O, F), BF),
        pltpu.VMEM((L, O, F), BF),
        pltpu.VMEM((L, O, F), BF),
        pltpu.VMEM((L, O, F), BF),
        pltpu.VMEM((L, O, F), BF),
        pltpu.VMEM((M, F), BF),
        pltpu.VMEM((F // NH, 2 * O), BF),
        pltpu.VMEM((F, N), F32),
        pltpu.VMEM((R - 1, F, O), BF),
        pltpu.VMEM((R - 1, F, O), BF),
        pltpu.VMEM((F, F), F32),
        pltpu.VMEM((R - 1, G, F), F32),
        pltpu.VMEM((steps, G, F), F32),
        pltpu.VMEM((steps, G, F), F32),
        pltpu.VMEM((F, F), F32),
        dma((NB,)),
        dma((R - 1,)), dma((R - 1,)),
        dma((C - 1,)), dma((C - 1,)),
        dma((NH, L)), dma((NH, L)),
        dma((NH, L)), dma((NH, L)),
        dma((NH, L)), dma((NH, L)),
        dma((NH, L)), dma((NH, L)),
        dma((NH, L)), dma((NH, L)),
        dma((NH, L)), dma((NH, L)),
        dma((NH, R - 1)), dma((NH, R - 1)),
        dma((R - 1,)), dma((R - 1,)),
        dma((steps,)), dma((steps,)),
        dma((R - 1,)), dma((R - 1,)),
    ]
    out, fgrad, wgrad = pl.pallas_call(
        functools.partial(kernel, R, C, scale),
        out_shape=(
            jax.ShapeDtypeStruct((O, F), BF),
            jax.ShapeDtypeStruct((O, F), BF),
            jax.ShapeDtypeStruct((F, F), F32),
        ),
        in_specs=[vmem, vmem, smem, smem, vmem, pl.BlockSpec(memory_space=pl.ANY)],
        out_specs=(vmem, vmem, vmem),
        scratch_shapes=scratch,
        compiler_params=pltpu.CompilerParams(
            collective_id=0, has_side_effects=True, vmem_limit_bytes=60 * 1024 * 1024),
    )(features, weight, tile_cols, tile_counts, cotangent, adjacency)
    return out, fgrad, wgrad


def solution(mesh):
    placed = (
        P(("col", "row"), None),
        P(),
        P("row", "col", None, None),
        P("row", "col"),
        P("row", "col"),
        P(("row", "col"), None),
    )
    return jax.shard_map(
        shards,
        mesh=mesh,
        in_specs=placed,
        out_specs=(P(("row", "col"), None), P(("col", "row"), None), P()),
        check_vma=False,
    )
```

```python
import functools
import math

import jax
import jax.numpy as jnp
from jax import lax
from jax.experimental import pallas as pl
from jax.experimental.pallas import tpu as pltpu
from jax.sharding import PartitionSpec as P

MESH = pl.DeviceIdType.MESH
BF = jnp.bfloat16
F32 = jnp.float32
NH = 2


def kernel(
    R, C, scale,
    feats, weight, cols, counts, cot, adj,
    out, fgrad, wgrad,
    adj_v, dense, hid, deg, deg_rx, part, pair_tx, pair_rx,
    in_r, in_l, tx_r, tx_l, slab, slab_t, ndt, nd_tx, nd_rx,
    w_term, w_rx, w_cur, w_in, w_all,
    adj_sem, h_send, h_recv, d_send, d_recv, p_send, p_recv,
    r_send, r_recv, l_send, l_recv, gr_send, gr_recv, gl_send, gl_recv,
    s_send, s_recv, n_send, n_recv,
    w_send, w_recv, b_send, b_recv, a_send, a_recv,
):
    r = lax.axis_index("row")
    c = lax.axis_index("col")
    L = C // 2
    z = c // 2
    k = c % 2
    NB, K, T, _ = adj.shape
    O, F = feats.shape
    N = O * R
    J = N // T
    HF = F // NH

    def cs(h):
        return slice(h * HF, (h + 1) * HF)

    sib = (r, 2 * z + 1 - k)
    right = (r, c + 2)
    left = (r, c - 2)

    def remote(src, dst, ss, rs, dev):
        return pltpu.make_async_remote_copy(
            src_ref=src, dst_ref=dst, send_sem=ss, recv_sem=rs,
            device_id=dev, device_id_type=MESH)

    def row_peer(d):
        return lax.rem(r + d, R)

    def col_peer(d):
        return lax.rem(c + d, C)

    def load_adj(b):
        return pltpu.make_async_copy(adj.at[b], adj_v.at[b], adj_sem.at[b])

    @pl.loop(0, NB)
    def _(b):
        load_adj(b).start()

    barrier = pltpu.get_barrier_semaphore()
    for d in range(1, R):
        pl.semaphore_signal(barrier, inc=1, device_id=(row_peer(d), c), device_id_type=MESH)
    for d in range(1, C):
        pl.semaphore_signal(barrier, inc=1, device_id=(r, col_peer(d)), device_id_type=MESH)

    hid[pl.ds(pl.multiple_of(r * O, O), O), :] = jnp.dot(
        feats[...], weight[...], preferred_element_type=F32).astype(BF)
    pl.semaphore_wait(barrier, R + C - 2)

    def h_copy(d):
        own = hid.at[pl.ds(pl.multiple_of(r * O, O), O), :]
        return remote(own, own, h_send.at[d - 1], h_recv.at[d - 1], (row_peer(d), c))

    for d in range(1, R):
        h_copy(d).start()

    @pl.loop(0, NB)
    def _(b):
        load_adj(b).wait()
        n = counts[b, 0]
        rows = pl.ds(pl.multiple_of(b * T, T), T)
        vals = []
        for s in range(K):
            live = jnp.where(s < n, 1.0, 0.0).astype(F32)
            v = adj_v[b, s].astype(F32) * live
            vals.append(v)
        total = functools.reduce(lambda a, e: a + e, vals)
        deg[:, rows] = lax.dot_general(
            jnp.ones((8, T), BF), total.astype(BF), (((1,), (1,)), ((), ())),
            preferred_element_type=F32)
        for j in range(J):
            acc = None
            for s in range(K):
                m = jnp.where(cols[b, s] == j, 1.0, 0.0).astype(F32)
                term = vals[s] * m
                acc = term if acc is None else acc + term
            dense[rows, j * T:(j + 1) * T] = acc.astype(BF)

    def d_copy(d):
        src = deg.at[:, pl.ds(pl.multiple_of(col_peer(d) * O, O), O)]
        return remote(src, deg_rx.at[d - 1], d_send.at[d - 1], d_recv.at[d - 1],
                      (r, col_peer(d)))

    for d in range(1, C):
        d_copy(d).start()

    for d in range(1, R):
        h_copy(d).wait_recv()

    per = 2 * O // T

    def p_copy(q, h):
        return remote(pair_tx.at[h, q], pair_rx.at[h, q],
                      p_send.at[h, q], p_recv.at[h, q], sib)

    def part_of(q, core):
        return pl.ds(pl.multiple_of((2 * q + core) * O, O), O)

    @pl.loop(0, L)
    def _(i):
        q = jnp.where(i % 2 == 0, L - 1 - i // 2, i // 2)
        for bb in range(per):
            rows = pl.ds(pl.multiple_of((q * per + bb) * T, T), T)
            part[rows, :] = jnp.dot(dense[rows, :], hid[...], preferred_element_type=F32)
        for h in range(NH):
            pair_tx[h, q] = part[part_of(q, 1 - k), cs(h)].astype(BF)
            p_copy(q, h).start()

    def r_copy(q, h):
        return remote(tx_r.at[h, q], in_r.at[h, q],
                      r_send.at[h, q], r_recv.at[h, q], right)

    def l_copy(q, h):
        return remote(tx_l.at[h, q], in_l.at[h, q],
                      l_send.at[h, q], l_recv.at[h, q], left)

    def sum_step(i, h):
        qr = L - 1 - i
        ql = i

        @pl.when(qr > z)
        def _():
            p_copy(qr, h).wait_recv()
            own = part_of(qr, k)
            part[own, cs(h)] += pair_rx[h, qr].astype(F32)

            @pl.when(z > 0)
            def _():
                r_copy(qr, h).wait_recv()
                part[own, cs(h)] += in_r[h, qr].astype(F32)

            tx_r[h, qr] = part[own, cs(h)].astype(BF)
            r_copy(qr, h).start()

        @pl.when(ql < z)
        def _():
            p_copy(ql, h).wait_recv()
            own = part_of(ql, k)
            part[own, cs(h)] += pair_rx[h, ql].astype(F32)

            @pl.when(z < L - 1)
            def _():
                l_copy(ql, h).wait_recv()
                part[own, cs(h)] += in_l[h, ql].astype(F32)

            tx_l[h, ql] = part[own, cs(h)].astype(BF)
            l_copy(ql, h).start()

    @pl.loop(0, L - 1)
    def _(i):
        sum_step(i, 0)

    for d in range(1, C):
        d_copy(d).wait_recv()
    degree = deg[:, pl.ds(pl.multiple_of(c * O, O), O)]
    for d in range(1, C):
        degree = degree + deg_rx[d - 1]
    inv = lax.rsqrt(1.0 + degree)
    inv = jnp.transpose(jnp.broadcast_to(inv[0:1, :], (128, O)))[:, 0:1]

    mine = part_of(z, k)

    def finish(h):
        p_copy(z, h).wait_recv()
        part[mine, cs(h)] += pair_rx[h, z].astype(F32)

        @pl.when(z > 0)
        def _():
            r_copy(z, h).wait_recv()
            part[mine, cs(h)] += in_r[h, z].astype(F32)

        @pl.when(z < L - 1)
        def _():
            l_copy(z, h).wait_recv()
            part[mine, cs(h)] += in_l[h, z].astype(F32)

        pre = part[mine, cs(h)] * inv
        sig = jax.nn.sigmoid(pre)
        out[:, cs(h)] = (pre * sig).astype(BF)
        slab[h, mine, :] = (
            cot[:, cs(h)].astype(F32) * sig * (1.0 + pre * (1.0 - sig)) * inv).astype(BF)

    def s_copy(p, h):
        ref = slab.at[h, part_of(p, k), :]
        return remote(ref, ref, s_send.at[h, p], s_recv.at[h, p], sib)

    def s_wait(p, h):
        ref = slab.at[h, part_of(p, 1 - k), :]
        remote(ref, ref, s_send.at[h, p], s_recv.at[h, p], sib).wait_recv()

    def gr_copy(i, p, h):
        ref = slab.at[h, part_of(p, k), :]
        return remote(ref, ref, gr_send.at[h, i], gr_recv.at[h, i], right)

    def gl_copy(i, p, h):
        ref = slab.at[h, part_of(p, k), :]
        return remote(ref, ref, gl_send.at[h, i], gl_recv.at[h, i], left)

    def spread(h):
        @pl.when(z < L - 1)
        def _():
            gr_copy(0, z, h).start()

        @pl.when(z > 0)
        def _():
            gl_copy(0, z, h).start()

        s_copy(z, h).start()

    def forward(i, h):
        pr = z - i
        pln = z + i

        @pl.when(pr >= 0)
        def _():
            gr_copy(i - 1, pr, h).wait_recv()

            @pl.when(z < L - 1)
            def _():
                gr_copy(i, pr, h).start()
            s_copy(pr, h).start()

        @pl.when(pln <= L - 1)
        def _():
            gl_copy(i - 1, pln, h).wait_recv()

            @pl.when(z > 0)
            def _():
                gl_copy(i, pln, h).start()
            s_copy(pln, h).start()

    CH = 512 if N % 512 == 0 else T

    def accumulate(p, h, first=False):
        rows = pl.ds(pl.multiple_of(2 * p * O, 2 * O), 2 * O)
        s_wait(p, h)
        slab_t[...] = jnp.transpose(slab[h, rows, :].astype(F32)).astype(BF)

        @pl.loop(0, N // CH)
        def _(j):
            cc = pl.ds(pl.multiple_of(j * CH, CH), CH)
            term = jnp.dot(slab_t[...], dense[rows, cc], preferred_element_type=F32)
            if first:
                ndt[cs(h), cc] = term
            else:
                ndt[cs(h), cc] += term

    def both(i, h):
        @pl.when(z - i >= 0)
        def _():
            accumulate(z - i, h)

        @pl.when(z + i <= L - 1)
        def _():
            accumulate(z + i, h)

    def n_copy(d, h):
        return remote(nd_tx.at[d - 1, cs(h), :], nd_rx.at[d - 1, cs(h), :],
                      n_send.at[h, d - 1], n_recv.at[h, d - 1], (row_peer(d), c))

    def scatter(h):
        for d in range(1, R):
            there = pl.ds(pl.multiple_of(row_peer(d) * O, O), O)
            nd_tx[d - 1, cs(h), :] = ndt[cs(h), there].astype(BF)
            n_copy(d, h).start()

    finish(0)
    spread(0)

    @pl.loop(0, L - 1)
    def _(i):
        sum_step(i, 1)
        forward(i + 1, 0)

    finish(1)
    spread(1)
    accumulate(z, 0, True)

    @pl.loop(1, L)
    def _(i):
        forward(i, 1)
        both(i, 0)

    scatter(0)
    accumulate(z, 1, True)

    @pl.loop(1, L)
    def _(i):
        both(i, 1)

    scatter(1)

    total = ndt[:, pl.ds(pl.multiple_of(r * O, O), O)]
    for d in range(1, R):
        for h in range(NH):
            n_copy(d, h).wait_recv()
        total = total + nd_rx[d - 1].astype(F32)
    node = jnp.transpose(total).astype(BF)
    w_term[...] = lax.dot_general(
        feats[...], node, (((0,), (0,)), ((), ())), preferred_element_type=F32)

    G = F // R
    steps = C.bit_length() - 1

    def w_rows(i):
        return pl.ds(pl.multiple_of(i * G, G), G)

    def w_copy(d):
        return remote(w_term.at[w_rows(row_peer(d)), :], w_rx.at[d - 1],
                      w_send.at[d - 1], w_recv.at[d - 1], (row_peer(d), c))

    def b_copy(s):
        w = 1 << s
        partner = c + w - 2 * w * ((c // w) % 2)
        return remote(w_cur.at[s], w_in.at[s], b_send.at[s], b_recv.at[s], (r, partner))

    def a_copy(d):
        ref = w_all.at[w_rows(r), :]
        return remote(ref, ref, a_send.at[d - 1], a_recv.at[d - 1], (row_peer(d), c))

    for d in range(1, R):
        w_copy(d).start()
    fgrad[...] = lax.dot_general(
        node, weight[...], (((1,), (1,)), ((), ())), preferred_element_type=F32).astype(BF)

    wsum = w_term[w_rows(r), :]
    for d in range(1, R):
        w_copy(d).wait_recv()
        wsum = wsum + w_rx[d - 1]
    for s in range(steps):
        w_cur[s] = wsum
        b_copy(s).start()
        b_copy(s).wait_recv()
        wsum = wsum + w_in[s]
    w_all[w_rows(r), :] = wsum * scale
    for d in range(1, R):
        a_copy(d).start()
    for d in range(1, R):
        a_copy(d).wait_recv()
    wgrad[...] = w_all[...]

    def drain(q, h):
        p_copy(q, h).wait_send()
        s_copy(q, h).wait_send()

        @pl.when(q > z)
        def _():
            r_copy(q, h).wait_send()

        @pl.when(q < z)
        def _():
            l_copy(q, h).wait_send()

        @pl.when((q <= z) & (z < L - 1))
        def _():
            gr_copy(q, z - q, h).wait_send()

        @pl.when((q <= L - 1 - z) & (z > 0))
        def _():
            gl_copy(q, z + q, h).wait_send()

    for s in range(steps):
        b_copy(s).wait_send()
    for d in range(1, R):
        w_copy(d).wait_send()
        a_copy(d).wait_send()
    for d in range(1, R):
        h_copy(d).wait_send()
        for h in range(NH):
            n_copy(d, h).wait_send()
    for d in range(1, C):
        d_copy(d).wait_send()

    @pl.loop(0, L)
    def _(q):
        for h in range(NH):
            drain(q, h)


def shards(features, weight, adjacency, tile_cols, tile_counts, cotangent):
    R = lax.axis_size("row")
    C = lax.axis_size("col")
    L = C // 2
    NB, K, T, _ = adjacency.shape
    O, F = features.shape
    N = O * R
    M = NB * T
    G = F // R
    steps = C.bit_length() - 1
    scale = 1.0 / math.sqrt(O * R * C)
    vmem = pl.BlockSpec(memory_space=pltpu.VMEM)
    smem = pl.BlockSpec(memory_space=pltpu.SMEM)
    dma = pltpu.SemaphoreType.DMA
    scratch = [
        pltpu.VMEM((NB, K, T, T), jnp.int32),
        pltpu.VMEM((M, N), BF),
        pltpu.VMEM((N, F), BF),
        pltpu.VMEM((8, M), F32),
        pltpu.VMEM((C - 1, 8, O), F32),
        pltpu.VMEM((M, F), F32),
        pltpu.VMEM((NH, L, O, F // NH), BF),
        pltpu.VMEM((NH, L, O, F // NH), BF),
        pltpu.VMEM((NH, L, O, F // NH), BF),
        pltpu.VMEM((NH, L, O, F // NH), BF),
        pltpu.VMEM((NH, L, O, F // NH), BF),
        pltpu.VMEM((NH, L, O, F // NH), BF),
        pltpu.VMEM((NH, M, F // NH), BF),
        pltpu.VMEM((F // NH, 2 * O), BF),
        pltpu.VMEM((F, N), F32),
        pltpu.VMEM((R - 1, F, O), BF),
        pltpu.VMEM((R - 1, F, O), BF),
        pltpu.VMEM((F, F), F32),
        pltpu.VMEM((R - 1, G, F), F32),
        pltpu.VMEM((steps, G, F), F32),
        pltpu.VMEM((steps, G, F), F32),
        pltpu.VMEM((F, F), F32),
        dma((NB,)),
        dma((R - 1,)), dma((R - 1,)),
        dma((C - 1,)), dma((C - 1,)),
        dma((NH, L)), dma((NH, L)),
        dma((NH, L)), dma((NH, L)),
        dma((NH, L)), dma((NH, L)),
        dma((NH, L)), dma((NH, L)),
        dma((NH, L)), dma((NH, L)),
        dma((NH, L)), dma((NH, L)),
        dma((NH, R - 1)), dma((NH, R - 1)),
        dma((R - 1,)), dma((R - 1,)),
        dma((steps,)), dma((steps,)),
        dma((R - 1,)), dma((R - 1,)),
    ]
    out, fgrad, wgrad = pl.pallas_call(
        functools.partial(kernel, R, C, scale),
        out_shape=(
            jax.ShapeDtypeStruct((O, F), BF),
            jax.ShapeDtypeStruct((O, F), BF),
            jax.ShapeDtypeStruct((F, F), F32),
        ),
        in_specs=[vmem, vmem, smem, smem, vmem, pl.BlockSpec(memory_space=pl.ANY)],
        out_specs=(vmem, vmem, vmem),
        scratch_shapes=scratch,
        compiler_params=pltpu.CompilerParams(
            collective_id=0, has_side_effects=True, vmem_limit_bytes=60 * 1024 * 1024),
    )(features, weight, tile_cols, tile_counts, cotangent, adjacency)
    return out, fgrad, wgrad


def solution(mesh):
    placed = (
        P(("col", "row"), None),
        P(),
        P("row", "col", None, None),
        P("row", "col"),
        P("row", "col"),
        P(("row", "col"), None),
    )
    return jax.shard_map(
        shards,
        mesh=mesh,
        in_specs=placed,
        out_specs=(P(("row", "col"), None), P(("col", "row"), None), P()),
        check_vma=False,
    )
```

```python
import functools
import math

import jax
import jax.numpy as jnp
from jax import lax
from jax.experimental import pallas as pl
from jax.experimental.pallas import tpu as pltpu
from jax.sharding import PartitionSpec as P

MESH = pl.DeviceIdType.MESH
BF = jnp.bfloat16
F32 = jnp.float32


def kernel(
    R, C, scale,
    feats, weight, cols, counts, cot, adj,
    out, fgrad, wgrad,
    adj_v, dense, hid, deg, deg_rx, part, pair_tx, pair_rx,
    in_r, in_l, tx_r, tx_l, slab, slab_t, ndt, nd_tx, nd_rx,
    w_term, w_tx, w_rx, w_cur, w_in, w_all,
    adj_sem, h_send, h_recv, d_send, d_recv, p_send, p_recv,
    r_send, r_recv, l_send, l_recv, gr_send, gr_recv, gl_send, gl_recv,
    s_send, s_recv, n_send, n_recv,
    w_send, w_recv, b_send, b_recv, a_send, a_recv,
):
    r = lax.axis_index("row")
    c = lax.axis_index("col")
    L = C // 2
    z = c // 2
    k = c % 2
    NB, K, T, _ = adj.shape
    O, F = feats.shape
    N = O * R
    J = N // T
    sib = (r, 2 * z + 1 - k)
    right = (r, c + 2)
    left = (r, c - 2)

    def remote(src, dst, ss, rs, dev):
        return pltpu.make_async_remote_copy(
            src_ref=src, dst_ref=dst, send_sem=ss, recv_sem=rs,
            device_id=dev, device_id_type=MESH)

    def row_peer(d):
        return lax.rem(r + d, R)

    def col_peer(d):
        return lax.rem(c + d, C)

    def load_adj(b):
        return pltpu.make_async_copy(adj.at[b], adj_v.at[b], adj_sem.at[b])

    @pl.loop(0, NB)
    def _(b):
        load_adj(b).start()

    barrier = pltpu.get_barrier_semaphore()
    for d in range(1, R):
        pl.semaphore_signal(barrier, inc=1, device_id=(row_peer(d), c), device_id_type=MESH)
    for d in range(1, C):
        pl.semaphore_signal(barrier, inc=1, device_id=(r, col_peer(d)), device_id_type=MESH)

    hid[pl.ds(pl.multiple_of(r * O, O), O), :] = jnp.dot(
        feats[...], weight[...], preferred_element_type=F32).astype(BF)
    pl.semaphore_wait(barrier, R + C - 2)

    def h_copy(d):
        own = hid.at[pl.ds(pl.multiple_of(r * O, O), O), :]
        return remote(own, own, h_send.at[d - 1], h_recv.at[d - 1], (row_peer(d), c))

    for d in range(1, R):
        h_copy(d).start()

    @pl.loop(0, NB)
    def _(b):
        load_adj(b).wait()
        n = counts[b, 0]
        rows = pl.ds(pl.multiple_of(b * T, T), T)
        vals = []
        for s in range(K):
            live = jnp.where(s < n, 1.0, 0.0).astype(F32)
            v = adj_v[b, s].astype(F32) * live
            vals.append(v)
        total = functools.reduce(lambda a, e: a + e, vals)
        deg[:, rows] = lax.dot_general(
            jnp.ones((8, T), BF), total.astype(BF), (((1,), (1,)), ((), ())),
            preferred_element_type=F32)
        for j in range(J):
            acc = None
            for s in range(K):
                m = jnp.where(cols[b, s] == j, 1.0, 0.0).astype(F32)
                term = vals[s] * m
                acc = term if acc is None else acc + term
            dense[rows, j * T:(j + 1) * T] = acc.astype(BF)

    def d_copy(d):
        src = deg.at[:, pl.ds(pl.multiple_of(col_peer(d) * O, O), O)]
        return remote(src, deg_rx.at[d - 1], d_send.at[d - 1], d_recv.at[d - 1],
                      (r, col_peer(d)))

    for d in range(1, C):
        d_copy(d).start()

    for d in range(1, R):
        h_copy(d).wait_recv()

    per = 2 * O // T

    def p_copy(q):
        return remote(pair_tx.at[q], pair_rx.at[q], p_send.at[q], p_recv.at[q], sib)

    def part_of(q, core):
        return pl.ds(pl.multiple_of((2 * q + core) * O, O), O)

    @pl.loop(0, L)
    def _(i):
        q = jnp.where(i % 2 == 0, L - 1 - i // 2, i // 2)
        for bb in range(per):
            rows = pl.ds(pl.multiple_of((q * per + bb) * T, T), T)
            part[rows, :] = jnp.dot(dense[rows, :], hid[...], preferred_element_type=F32)
        pair_tx[q] = part[part_of(q, 1 - k), :].astype(BF)
        p_copy(q).start()

    def r_copy(q):
        return remote(tx_r.at[q], in_r.at[q], r_send.at[q], r_recv.at[q], right)

    def l_copy(q):
        return remote(tx_l.at[q], in_l.at[q], l_send.at[q], l_recv.at[q], left)

    @pl.loop(0, L - 1)
    def _(i):
        qr = L - 1 - i
        ql = i

        @pl.when(qr > z)
        def _():
            p_copy(qr).wait_recv()
            own = part_of(qr, k)
            part[own, :] += pair_rx[qr].astype(F32)

            @pl.when(z > 0)
            def _():
                r_copy(qr).wait_recv()
                part[own, :] += in_r[qr].astype(F32)

            tx_r[qr] = part[own, :].astype(BF)
            r_copy(qr).start()

        @pl.when(ql < z)
        def _():
            p_copy(ql).wait_recv()
            own = part_of(ql, k)
            part[own, :] += pair_rx[ql].astype(F32)

            @pl.when(z < L - 1)
            def _():
                l_copy(ql).wait_recv()
                part[own, :] += in_l[ql].astype(F32)

            tx_l[ql] = part[own, :].astype(BF)
            l_copy(ql).start()

    for d in range(1, C):
        d_copy(d).wait_recv()
    degree = deg[:, pl.ds(pl.multiple_of(c * O, O), O)]
    for d in range(1, C):
        degree = degree + deg_rx[d - 1]
    inv = lax.rsqrt(1.0 + degree)
    inv = jnp.transpose(jnp.broadcast_to(inv[0:1, :], (128, O)))[:, 0:1]

    mine = part_of(z, k)
    p_copy(z).wait_recv()
    part[mine, :] += pair_rx[z].astype(F32)

    @pl.when(z > 0)
    def _():
        r_copy(z).wait_recv()
        part[mine, :] += in_r[z].astype(F32)

    @pl.when(z < L - 1)
    def _():
        l_copy(z).wait_recv()
        part[mine, :] += in_l[z].astype(F32)

    pre = part[mine, :] * inv
    sig = jax.nn.sigmoid(pre)
    out[...] = (pre * sig).astype(BF)
    slab[mine, :] = (cot[...].astype(F32) * sig * (1.0 + pre * (1.0 - sig)) * inv).astype(BF)

    def s_copy(p):
        ref = slab.at[part_of(p, k), :]
        return remote(ref, ref, s_send.at[p], s_recv.at[p], sib)

    def s_wait(p):
        ref = slab.at[part_of(p, 1 - k), :]
        remote(ref, ref, s_send.at[p], s_recv.at[p], sib).wait_recv()

    def gr_copy(i, p):
        ref = slab.at[part_of(p, k), :]
        return remote(ref, ref, gr_send.at[i], gr_recv.at[i], right)

    def gl_copy(i, p):
        ref = slab.at[part_of(p, k), :]
        return remote(ref, ref, gl_send.at[i], gl_recv.at[i], left)

    @pl.when(z < L - 1)
    def _():
        gr_copy(0, z).start()

    @pl.when(z > 0)
    def _():
        gl_copy(0, z).start()

    s_copy(z).start()
    CH = 512 if N % 512 == 0 else T
    ndt[...] = jnp.zeros_like(ndt)

    def accumulate(p):
        rows = pl.ds(pl.multiple_of(2 * p * O, 2 * O), 2 * O)
        slab_t[...] = jnp.transpose(slab[rows, :].astype(F32)).astype(BF)

        @pl.loop(0, N // CH)
        def _(j):
            cc = pl.ds(pl.multiple_of(j * CH, CH), CH)
            ndt[:, cc] += jnp.dot(slab_t[...], dense[rows, cc], preferred_element_type=F32)

    s_wait(z)
    accumulate(z)

    @pl.loop(1, L)
    def _(i):
        pr = z - i
        pln = z + i

        @pl.when(pr >= 0)
        def _():
            gr_copy(i - 1, pr).wait_recv()

            @pl.when(z < L - 1)
            def _():
                gr_copy(i, pr).start()
            s_copy(pr).start()

        @pl.when(pln <= L - 1)
        def _():
            gl_copy(i - 1, pln).wait_recv()

            @pl.when(z > 0)
            def _():
                gl_copy(i, pln).start()
            s_copy(pln).start()

        @pl.when(pr >= 0)
        def _():
            s_wait(pr)
            accumulate(pr)

        @pl.when(pln <= L - 1)
        def _():
            s_wait(pln)
            accumulate(pln)

    def n_copy(d):
        return remote(nd_tx.at[d - 1], nd_rx.at[d - 1], n_send.at[d - 1], n_recv.at[d - 1],
                      (row_peer(d), c))

    for d in range(1, R):
        nd_tx[d - 1] = ndt[:, pl.ds(pl.multiple_of(row_peer(d) * O, O), O)].astype(BF)
        n_copy(d).start()
    total = ndt[:, pl.ds(pl.multiple_of(r * O, O), O)]
    for d in range(1, R):
        n_copy(d).wait_recv()
        total = total + nd_rx[d - 1].astype(F32)
    node = jnp.transpose(total).astype(BF)
    w_term[...] = lax.dot_general(
        feats[...], node, (((0,), (0,)), ((), ())), preferred_element_type=F32)

    G = F // R
    steps = C.bit_length() - 1

    def w_rows(i):
        return pl.ds(pl.multiple_of(i * G, G), G)

    def w_copy(d):
        return remote(w_tx.at[w_rows(row_peer(d)), :], w_rx.at[d - 1],
                      w_send.at[d - 1], w_recv.at[d - 1], (row_peer(d), c))

    def b_copy(s):
        w = 1 << s
        partner = c + w - 2 * w * ((c // w) % 2)
        return remote(w_cur.at[s], w_in.at[s], b_send.at[s], b_recv.at[s], (r, partner))

    def a_copy(d):
        ref = w_all.at[w_rows(r), :]
        return remote(ref, ref, a_send.at[d - 1], a_recv.at[d - 1], (row_peer(d), c))

    w_tx[...] = w_term[...].astype(BF)
    for d in range(1, R):
        w_copy(d).start()
    fgrad[...] = lax.dot_general(
        node, weight[...], (((1,), (1,)), ((), ())), preferred_element_type=F32).astype(BF)

    wsum = w_term[w_rows(r), :]
    for d in range(1, R):
        w_copy(d).wait_recv()
        wsum = wsum + w_rx[d - 1].astype(F32)
    for s in range(steps):
        w_cur[s] = wsum
        b_copy(s).start()
        b_copy(s).wait_recv()
        wsum = wsum + w_in[s]
    w_all[w_rows(r), :] = wsum * scale
    for d in range(1, R):
        a_copy(d).start()
    for d in range(1, R):
        a_copy(d).wait_recv()
    wgrad[...] = w_all[...]

    for s in range(steps):
        b_copy(s).wait_send()
    for d in range(1, R):
        w_copy(d).wait_send()
        a_copy(d).wait_send()
    for d in range(1, R):
        h_copy(d).wait_send()
        n_copy(d).wait_send()
    for d in range(1, C):
        d_copy(d).wait_send()

    @pl.loop(0, L)
    def _(q):
        p_copy(q).wait_send()
        s_copy(q).wait_send()

        @pl.when(q > z)
        def _():
            r_copy(q).wait_send()

        @pl.when(q < z)
        def _():
            l_copy(q).wait_send()

        @pl.when((q <= z) & (z < L - 1))
        def _():
            gr_copy(q, z - q).wait_send()

        @pl.when((q <= L - 1 - z) & (z > 0))
        def _():
            gl_copy(q, z + q).wait_send()


def shards(features, weight, adjacency, tile_cols, tile_counts, cotangent):
    R = lax.axis_size("row")
    C = lax.axis_size("col")
    L = C // 2
    NB, K, T, _ = adjacency.shape
    O, F = features.shape
    N = O * R
    M = NB * T
    G = F // R
    steps = C.bit_length() - 1
    scale = 1.0 / math.sqrt(O * R * C)
    vmem = pl.BlockSpec(memory_space=pltpu.VMEM)
    smem = pl.BlockSpec(memory_space=pltpu.SMEM)
    dma = pltpu.SemaphoreType.DMA
    scratch = [
        pltpu.VMEM((NB, K, T, T), jnp.int32),
        pltpu.VMEM((M, N), BF),
        pltpu.VMEM((N, F), BF),
        pltpu.VMEM((8, M), F32),
        pltpu.VMEM((C - 1, 8, O), F32),
        pltpu.VMEM((M, F), F32),
        pltpu.VMEM((L, O, F), BF),
        pltpu.VMEM((L, O, F), BF),
        pltpu.VMEM((L, O, F), BF),
        pltpu.VMEM((L, O, F), BF),
        pltpu.VMEM((L, O, F), BF),
        pltpu.VMEM((L, O, F), BF),
        pltpu.VMEM((M, F), BF),
        pltpu.VMEM((F, 2 * O), BF),
        pltpu.VMEM((F, N), F32),
        pltpu.VMEM((R - 1, F, O), BF),
        pltpu.VMEM((R - 1, F, O), BF),
        pltpu.VMEM((F, F), F32),
        pltpu.VMEM((F, F), BF),
        pltpu.VMEM((R - 1, G, F), BF),
        pltpu.VMEM((steps, G, F), F32),
        pltpu.VMEM((steps, G, F), F32),
        pltpu.VMEM((F, F), F32),
        dma((NB,)),
        dma((R - 1,)), dma((R - 1,)),
        dma((C - 1,)), dma((C - 1,)),
        dma((L,)), dma((L,)),
        dma((L,)), dma((L,)),
        dma((L,)), dma((L,)),
        dma((L,)), dma((L,)),
        dma((L,)), dma((L,)),
        dma((L,)), dma((L,)),
        dma((R - 1,)), dma((R - 1,)),
        dma((R - 1,)), dma((R - 1,)),
        dma((steps,)), dma((steps,)),
        dma((R - 1,)), dma((R - 1,)),
    ]
    out, fgrad, wgrad = pl.pallas_call(
        functools.partial(kernel, R, C, scale),
        out_shape=(
            jax.ShapeDtypeStruct((O, F), BF),
            jax.ShapeDtypeStruct((O, F), BF),
            jax.ShapeDtypeStruct((F, F), F32),
        ),
        in_specs=[vmem, vmem, smem, smem, vmem, pl.BlockSpec(memory_space=pl.ANY)],
        out_specs=(vmem, vmem, vmem),
        scratch_shapes=scratch,
        compiler_params=pltpu.CompilerParams(
            collective_id=0, has_side_effects=True, vmem_limit_bytes=60 * 1024 * 1024),
    )(features, weight, tile_cols, tile_counts, cotangent, adjacency)
    return out, fgrad, wgrad


def solution(mesh):
    placed = (
        P(("col", "row"), None),
        P(),
        P("row", "col", None, None),
        P("row", "col"),
        P("row", "col"),
        P(("row", "col"), None),
    )
    return jax.shard_map(
        shards,
        mesh=mesh,
        in_specs=placed,
        out_specs=(P(("row", "col"), None), P(("col", "row"), None), P()),
        check_vma=False,
    )
```

```python
import functools
import math

import jax
import jax.numpy as jnp
from jax import lax
from jax.experimental import pallas as pl
from jax.experimental.pallas import tpu as pltpu
from jax.sharding import PartitionSpec as P

MESH = pl.DeviceIdType.MESH
BF = jnp.bfloat16
F32 = jnp.float32


def kernel(
    R, C, scale,
    feats, weight, cols, counts, cot, adj,
    out, fgrad, wgrad,
    adj_v, dense, hid, deg, deg_rx, part, pair_tx, pair_rx,
    in_r, in_l, tx_r, tx_l, slab, slab_t, ndt, nd_tx, nd_rx,
    w_term, w_tx, w_rx, w_cur, w_in, w_all,
    adj_sem, h_send, h_recv, d_send, d_recv, p_send, p_recv,
    r_send, r_recv, l_send, l_recv, gr_send, gr_recv, gl_send, gl_recv,
    s_send, s_recv, n_send, n_recv,
    w_send, w_recv, b_send, b_recv, a_send, a_recv,
):
    r = lax.axis_index("row")
    c = lax.axis_index("col")
    L = C // 2
    z = c // 2
    k = c % 2
    NB, K, T, _ = adj.shape
    O, F = feats.shape
    N = O * R
    J = N // T
    sib = (r, 2 * z + 1 - k)
    right = (r, c + 2)
    left = (r, c - 2)

    def remote(src, dst, ss, rs, dev):
        return pltpu.make_async_remote_copy(
            src_ref=src, dst_ref=dst, send_sem=ss, recv_sem=rs,
            device_id=dev, device_id_type=MESH)

    def row_peer(d):
        return lax.rem(r + d, R)

    def col_peer(d):
        return lax.rem(c + d, C)

    def load_adj(b):
        return pltpu.make_async_copy(adj.at[b], adj_v.at[b], adj_sem.at[b])

    @pl.loop(0, NB)
    def _(b):
        load_adj(b).start()

    barrier = pltpu.get_barrier_semaphore()
    for d in range(1, R):
        pl.semaphore_signal(barrier, inc=1, device_id=(row_peer(d), c), device_id_type=MESH)
    for d in range(1, C):
        pl.semaphore_signal(barrier, inc=1, device_id=(r, col_peer(d)), device_id_type=MESH)

    hid[pl.ds(pl.multiple_of(r * O, O), O), :] = jnp.dot(
        feats[...], weight[...], preferred_element_type=F32).astype(BF)
    pl.semaphore_wait(barrier, R + C - 2)

    def h_copy(d):
        own = hid.at[pl.ds(pl.multiple_of(r * O, O), O), :]
        return remote(own, own, h_send.at[d - 1], h_recv.at[d - 1], (row_peer(d), c))

    for d in range(1, R):
        h_copy(d).start()

    @pl.loop(0, NB)
    def _(b):
        load_adj(b).wait()
        n = counts[b, 0]
        rows = pl.ds(pl.multiple_of(b * T, T), T)
        vals = []
        for s in range(K):
            live = jnp.where(s < n, 1.0, 0.0).astype(F32)
            v = adj_v[b, s].astype(F32) * live
            vals.append(v)
        total = functools.reduce(lambda a, e: a + e, vals)
        deg[:, rows] = lax.dot_general(
            jnp.ones((8, T), BF), total.astype(BF), (((1,), (1,)), ((), ())),
            preferred_element_type=F32)
        for j in range(J):
            acc = None
            for s in range(K):
                m = jnp.where(cols[b, s] == j, 1.0, 0.0).astype(F32)
                term = vals[s] * m
                acc = term if acc is None else acc + term
            dense[rows, j * T:(j + 1) * T] = acc.astype(BF)

    def d_copy(d):
        src = deg.at[:, pl.ds(pl.multiple_of(col_peer(d) * O, O), O)]
        return remote(src, deg_rx.at[d - 1], d_send.at[d - 1], d_recv.at[d - 1],
                      (r, col_peer(d)))

    for d in range(1, C):
        d_copy(d).start()

    for d in range(1, R):
        h_copy(d).wait_recv()

    per = 2 * O // T

    def p_copy(q):
        return remote(pair_tx.at[q], pair_rx.at[q], p_send.at[q], p_recv.at[q], sib)

    def part_of(q, core):
        return pl.ds(pl.multiple_of((2 * q + core) * O, O), O)

    @pl.loop(0, L)
    def _(i):
        q = jnp.where(i % 2 == 0, L - 1 - i // 2, i // 2)
        for bb in range(per):
            rows = pl.ds(pl.multiple_of((q * per + bb) * T, T), T)
            part[rows, :] = jnp.dot(dense[rows, :], hid[...], preferred_element_type=F32)
        pair_tx[q] = part[part_of(q, 1 - k), :].astype(BF)
        p_copy(q).start()

    def r_copy(q):
        return remote(tx_r.at[q], in_r.at[q], r_send.at[q], r_recv.at[q], right)

    def l_copy(q):
        return remote(tx_l.at[q], in_l.at[q], l_send.at[q], l_recv.at[q], left)

    @pl.loop(0, L - 1)
    def _(i):
        qr = L - 1 - i
        ql = i

        @pl.when(qr > z)
        def _():
            p_copy(qr).wait_recv()
            own = part_of(qr, k)
            part[own, :] += pair_rx[qr].astype(F32)

            @pl.when(z > 0)
            def _():
                r_copy(qr).wait_recv()
                part[own, :] += in_r[qr].astype(F32)

            tx_r[qr] = part[own, :].astype(BF)
            r_copy(qr).start()

        @pl.when(ql < z)
        def _():
            p_copy(ql).wait_recv()
            own = part_of(ql, k)
            part[own, :] += pair_rx[ql].astype(F32)

            @pl.when(z < L - 1)
            def _():
                l_copy(ql).wait_recv()
                part[own, :] += in_l[ql].astype(F32)

            tx_l[ql] = part[own, :].astype(BF)
            l_copy(ql).start()

    for d in range(1, C):
        d_copy(d).wait_recv()
    degree = deg[:, pl.ds(pl.multiple_of(c * O, O), O)]
    for d in range(1, C):
        degree = degree + deg_rx[d - 1]
    inv = lax.rsqrt(1.0 + degree)
    inv = jnp.transpose(jnp.broadcast_to(inv[0:1, :], (128, O)))[:, 0:1]

    mine = part_of(z, k)
    p_copy(z).wait_recv()
    part[mine, :] += pair_rx[z].astype(F32)

    @pl.when(z > 0)
    def _():
        r_copy(z).wait_recv()
        part[mine, :] += in_r[z].astype(F32)

    @pl.when(z < L - 1)
    def _():
        l_copy(z).wait_recv()
        part[mine, :] += in_l[z].astype(F32)

    pre = part[mine, :] * inv
    sig = jax.nn.sigmoid(pre)
    out[...] = (pre * sig).astype(BF)
    slab[mine, :] = (cot[...].astype(F32) * sig * (1.0 + pre * (1.0 - sig)) * inv).astype(BF)

    def s_copy(p):
        ref = slab.at[part_of(p, k), :]
        return remote(ref, ref, s_send.at[p], s_recv.at[p], sib)

    def s_wait(p):
        ref = slab.at[part_of(p, 1 - k), :]
        remote(ref, ref, s_send.at[p], s_recv.at[p], sib).wait_recv()

    def gr_copy(i, p):
        ref = slab.at[part_of(p, k), :]
        return remote(ref, ref, gr_send.at[i], gr_recv.at[i], right)

    def gl_copy(i, p):
        ref = slab.at[part_of(p, k), :]
        return remote(ref, ref, gl_send.at[i], gl_recv.at[i], left)

    @pl.when(z < L - 1)
    def _():
        gr_copy(0, z).start()

    @pl.when(z > 0)
    def _():
        gl_copy(0, z).start()

    s_copy(z).start()
    CH = 512 if N % 512 == 0 else T
    ndt[...] = jnp.zeros_like(ndt)

    def accumulate(p):
        rows = pl.ds(pl.multiple_of(2 * p * O, 2 * O), 2 * O)
        slab_t[...] = jnp.transpose(slab[rows, :].astype(F32)).astype(BF)

        @pl.loop(0, N // CH)
        def _(j):
            cc = pl.ds(pl.multiple_of(j * CH, CH), CH)
            ndt[:, cc] += jnp.dot(slab_t[...], dense[rows, cc], preferred_element_type=F32)

    s_wait(z)
    accumulate(z)

    @pl.loop(1, L)
    def _(i):
        pr = z - i
        pln = z + i

        @pl.when(pr >= 0)
        def _():
            gr_copy(i - 1, pr).wait_recv()

            @pl.when(z < L - 1)
            def _():
                gr_copy(i, pr).start()
            s_copy(pr).start()

        @pl.when(pln <= L - 1)
        def _():
            gl_copy(i - 1, pln).wait_recv()

            @pl.when(z > 0)
            def _():
                gl_copy(i, pln).start()
            s_copy(pln).start()

        @pl.when(pr >= 0)
        def _():
            s_wait(pr)
            accumulate(pr)

        @pl.when(pln <= L - 1)
        def _():
            s_wait(pln)
            accumulate(pln)

    def n_copy(d):
        return remote(nd_tx.at[d - 1], nd_rx.at[d - 1], n_send.at[d - 1], n_recv.at[d - 1],
                      (row_peer(d), c))

    for d in range(1, R):
        nd_tx[d - 1] = ndt[:, pl.ds(pl.multiple_of(row_peer(d) * O, O), O)].astype(BF)
        n_copy(d).start()
    total = ndt[:, pl.ds(pl.multiple_of(r * O, O), O)]
    for d in range(1, R):
        n_copy(d).wait_recv()
        total = total + nd_rx[d - 1].astype(F32)
    node = jnp.transpose(total).astype(BF)
    w_term[...] = lax.dot_general(
        feats[...], node, (((0,), (0,)), ((), ())), preferred_element_type=F32)

    G = F // R
    steps = C.bit_length() - 1

    def w_rows(i):
        return pl.ds(pl.multiple_of(i * G, G), G)

    def w_copy(d):
        return remote(w_tx.at[w_rows(row_peer(d)), :], w_rx.at[d - 1],
                      w_send.at[d - 1], w_recv.at[d - 1], (row_peer(d), c))

    def b_copy(s):
        w = 1 << s
        partner = c + w - 2 * w * ((c // w) % 2)
        return remote(w_cur.at[s], w_in.at[s], b_send.at[s], b_recv.at[s], (r, partner))

    def a_copy(d):
        ref = w_all.at[w_rows(r), :]
        return remote(ref, ref, a_send.at[d - 1], a_recv.at[d - 1], (row_peer(d), c))

    w_tx[...] = w_term[...].astype(BF)
    for d in range(1, R):
        w_copy(d).start()
    fgrad[...] = lax.dot_general(
        node, weight[...], (((1,), (1,)), ((), ())), preferred_element_type=F32).astype(BF)

    wsum = w_term[w_rows(r), :]
    for d in range(1, R):
        w_copy(d).wait_recv()
        wsum = wsum + w_rx[d - 1].astype(F32)
    for s in range(steps):
        w_cur[s] = wsum
        b_copy(s).start()
        b_copy(s).wait_recv()
        wsum = wsum + w_in[s]
    w_all[w_rows(r), :] = (wsum * scale).astype(BF)
    for d in range(1, R):
        a_copy(d).start()
    for d in range(1, R):
        a_copy(d).wait_recv()
    wgrad[...] = w_all[...].astype(F32)

    for s in range(steps):
        b_copy(s).wait_send()
    for d in range(1, R):
        w_copy(d).wait_send()
        a_copy(d).wait_send()
    for d in range(1, R):
        h_copy(d).wait_send()
        n_copy(d).wait_send()
    for d in range(1, C):
        d_copy(d).wait_send()

    @pl.loop(0, L)
    def _(q):
        p_copy(q).wait_send()
        s_copy(q).wait_send()

        @pl.when(q > z)
        def _():
            r_copy(q).wait_send()

        @pl.when(q < z)
        def _():
            l_copy(q).wait_send()

        @pl.when((q <= z) & (z < L - 1))
        def _():
            gr_copy(q, z - q).wait_send()

        @pl.when((q <= L - 1 - z) & (z > 0))
        def _():
            gl_copy(q, z + q).wait_send()


def shards(features, weight, adjacency, tile_cols, tile_counts, cotangent):
    R = lax.axis_size("row")
    C = lax.axis_size("col")
    L = C // 2
    NB, K, T, _ = adjacency.shape
    O, F = features.shape
    N = O * R
    M = NB * T
    G = F // R
    steps = C.bit_length() - 1
    scale = 1.0 / math.sqrt(O * R * C)
    vmem = pl.BlockSpec(memory_space=pltpu.VMEM)
    smem = pl.BlockSpec(memory_space=pltpu.SMEM)
    dma = pltpu.SemaphoreType.DMA
    scratch = [
        pltpu.VMEM((NB, K, T, T), jnp.int32),
        pltpu.VMEM((M, N), BF),
        pltpu.VMEM((N, F), BF),
        pltpu.VMEM((8, M), F32),
        pltpu.VMEM((C - 1, 8, O), F32),
        pltpu.VMEM((M, F), F32),
        pltpu.VMEM((L, O, F), BF),
        pltpu.VMEM((L, O, F), BF),
        pltpu.VMEM((L, O, F), BF),
        pltpu.VMEM((L, O, F), BF),
        pltpu.VMEM((L, O, F), BF),
        pltpu.VMEM((L, O, F), BF),
        pltpu.VMEM((M, F), BF),
        pltpu.VMEM((F, 2 * O), BF),
        pltpu.VMEM((F, N), F32),
        pltpu.VMEM((R - 1, F, O), BF),
        pltpu.VMEM((R - 1, F, O), BF),
        pltpu.VMEM((F, F), F32),
        pltpu.VMEM((F, F), BF),
        pltpu.VMEM((R - 1, G, F), BF),
        pltpu.VMEM((steps, G, F), F32),
        pltpu.VMEM((steps, G, F), F32),
        pltpu.VMEM((F, F), BF),
        dma((NB,)),
        dma((R - 1,)), dma((R - 1,)),
        dma((C - 1,)), dma((C - 1,)),
        dma((L,)), dma((L,)),
        dma((L,)), dma((L,)),
        dma((L,)), dma((L,)),
        dma((L,)), dma((L,)),
        dma((L,)), dma((L,)),
        dma((L,)), dma((L,)),
        dma((R - 1,)), dma((R - 1,)),
        dma((R - 1,)), dma((R - 1,)),
        dma((steps,)), dma((steps,)),
        dma((R - 1,)), dma((R - 1,)),
    ]
    out, fgrad, wgrad = pl.pallas_call(
        functools.partial(kernel, R, C, scale),
        out_shape=(
            jax.ShapeDtypeStruct((O, F), BF),
            jax.ShapeDtypeStruct((O, F), BF),
            jax.ShapeDtypeStruct((F, F), F32),
        ),
        in_specs=[vmem, vmem, smem, smem, vmem, pl.BlockSpec(memory_space=pl.ANY)],
        out_specs=(vmem, vmem, vmem),
        scratch_shapes=scratch,
        compiler_params=pltpu.CompilerParams(
            collective_id=0, has_side_effects=True, vmem_limit_bytes=60 * 1024 * 1024),
    )(features, weight, tile_cols, tile_counts, cotangent, adjacency)
    return out, fgrad, wgrad


def solution(mesh):
    placed = (
        P(("col", "row"), None),
        P(),
        P("row", "col", None, None),
        P("row", "col"),
        P("row", "col"),
        P(("row", "col"), None),
    )
    return jax.shard_map(
        shards,
        mesh=mesh,
        in_specs=placed,
        out_specs=(P(("row", "col"), None), P(("col", "row"), None), P()),
        check_vma=False,
    )
```
